256 devices in a mesh: grp: 4 (over z_hi), wr: 64 (over y, x, z_lo, core).
Axes of the slice: x: 4, y: 4, z: 8 (z_hi: 4, z_lo: 2; z = z_hi * 2 + z_lo), core: 2. Of those that a mesh axis runs over, the one named last changes fastest.
Arguments:
- snapshots: float32 [256, 1048576], P('wr', 'grp'), may hold values from -1300 to 1300
Outputs:
- basis: float32 [256, 1048576], P(None, ('grp', 'wr'))
- r_scaled: float32 [256, 256], P(None, 'wr')
The draws below stay inside these ranges and needn't reach their ends.
All inputs are finite; a program needn't handle non-finite values.
Results may differ from the reference program's by a relative error of at most 0.000073.
Values sent between devices are 32-bit elements; how exact they have to be, the bound alone decides.
A program may use at most 64 MiB of HBM per device.

```python
import math
import jax
import jax.numpy as jnp
from jax import lax

SNAP = 256
CELLS = 1048576


def draw_snapshots(key, part):
    keys = jax.random.split(key, 3)
    cells = jnp.arange(CELLS, dtype=jnp.float32)
    rise = 1.0 + 2.0 * cells / CELLS
    cell_scale = jnp.exp(jax.random.uniform(keys[1], (CELLS,), jnp.float32) * math.log(10.0)) * rise
    snap_scale = jnp.exp(jax.random.uniform(keys[2], (SNAP, 1), jnp.float32) * math.log(10.0))
    noise = jnp.clip(jax.random.normal(keys[0], (SNAP, CELLS), jnp.float32), -4.0, 4.0)
    values = cell_scale * snap_scale * noise
    return values.astype(jnp.float32)


def setup_inputs(seed: int = 0) -> dict:
    streams_of = jax.random.split(jax.random.key(seed), 2)
    return {
        "snapshots": draw_snapshots(jax.random.fold_in(streams_of[1], 71), 0),
    }


def reference(snapshots):
    gram = lax.dot_general(snapshots.astype(jnp.float32), snapshots.astype(jnp.float32), (((1,), (1,)), ((), ())), precision=lax.Precision.HIGHEST, preferred_element_type=jnp.float32)
    lower = jnp.linalg.cholesky(gram)
    solved = lax.linalg.triangular_solve(lower, snapshots, left_side=True, lower=True)
    scale = jnp.sqrt(jnp.float32(CELLS))
    return (solved * scale, lower.T / scale)
```

```python
import functools

import jax
import jax.numpy as jnp
from jax import lax
from jax.experimental import pallas as pl
from jax.experimental.pallas import tpu as pltpu
from jax.sharding import PartitionSpec as P

F32 = jnp.float32
BF = jnp.bfloat16
MESH = pl.DeviceIdType.MESH

def split3(v):
    hi=v.astype(BF); r=v-hi.astype(F32); mid=r.astype(BF); lo=(r-mid.astype(F32)).astype(BF)
    return hi,mid,lo

def rsqrt_exact(d):
    y=lax.rsqrt(d)
    return y*(1.5-0.5*d*y*y)

def factor(a_ref, v_ref, u_ref, b):
    n=a_ref.shape[0]; halves=n//128; groups=b//8
    lane=lax.broadcasted_iota(jnp.int32,(8,128),1); row=lax.broadcasted_iota(jnp.int32,(8,128),0)
    lane_all=lax.broadcasted_iota(jnp.int32,(n,n),1)
    lane_b=lax.broadcasted_iota(jnp.int32,(b,n),1); row_b=lax.broadcasted_iota(jnp.int32,(b,n),0)
    def panel(p,carry):
        k=pl.multiple_of(p*b,b)
        P=pltpu.roll(a_ref[pl.ds(k,b),:],lax.rem(n-k,n),1)
        G=[[P[8*g:8*g+8,128*h:128*h+128] for h in range(halves)] for g in range(groups)]
        UD=[None]*groups
        for q in range(groups):
            W=[{g:jnp.broadcast_to(G[g][0][:,8*q+j:8*q+j+1],(8,128)) for g in range(q,groups)} for j in range(8)]
            own=(lane>=8*q)&(lane<8*q+8)
            for g in range(q,groups):
                G[g][0]=jnp.where(own,(jnp.where(lane==row+8*q,1.0,0.0) if g==q else 0.0),G[g][0])
            dv=jnp.ones((8,128),F32)
            for j in range(8):
                d=W[j][q][j:j+1,:]
                r=1.0/d
                dv=jnp.where(row==j,d,dv)
                m={g:W[j][g]*r for g in range(q,groups)}
                m[q]=jnp.where(row>j,m[q],0.0)
                for jj in range(j+1,8):
                    pv=W[jj][q][j:j+1,:]
                    for g in range(q,groups): W[jj][g]=W[jj][g]-m[g]*pv
                pr=[G[q][h][j:j+1,:] for h in range(halves)]
                for g in range(q,groups):
                    for h in range(halves): G[g][h]=G[g][h]-m[g]*pr[h]
            s=rsqrt_exact(dv)
            ud=jnp.zeros((8,128),F32)
            for j in range(8): ud=jnp.where((lane==8*q+j)&(row<=j),W[j][q],ud)
            UD[q]=ud*s
            for h in range(halves): G[q][h]=G[q][h]*s
        Pf=jnp.concatenate([jnp.concatenate(g,axis=1) for g in G],axis=0)
        Pn=pltpu.roll(Pf,k,1)
        h3,m3,l3=split3(jnp.where((lane_b>row_b+k)&(lane_b<k+b),0.0,Pn))
        A=jnp.concatenate([h3,h3,m3,h3,l3,m3],axis=0)
        B=jnp.concatenate([h3,m3,h3,l3,h3,m3],axis=0)
        upd=lax.dot_general(A,B,(((0,),(0,)),((),())),preferred_element_type=F32)
        inpan=(lane_all>=k)&(lane_all<k+b)
        a_ref[...]=jnp.where(inpan,0.0,a_ref[...])-upd
        blk=(row_b//8)*8
        v_ref[pl.ds(k,b),:]=jnp.where(lane_b<=row_b+k,Pn,0.0)
        UDp=jnp.concatenate([jnp.concatenate([UD[g]]+[jnp.zeros((8,128),F32)]*(halves-1),axis=1) for g in range(groups)],axis=0)
        UDn=pltpu.roll(UDp,k,1)
        u_ref[pl.ds(k,b),:]=jnp.where(lane_b>=blk+k+8,Pn,UDn)
        return carry
    lax.fori_loop(0,n//b,panel,0)

def finish_kernel(b,cw,nz,g_ref,x_hbm,o_hbm,r_ref,a,v,u,xb,ob,xs,os):
    n,cells=x_hbm.shape; nch=cells//cw
    w=lax.axis_index("wr")
    loads=[pltpu.make_async_copy(x_hbm.at[:,pl.ds(i*cw,cw)],xb.at[:,pl.ds(i*cw,cw)],xs.at[i]) for i in range(nch)]
    for c in loads: c.start()
    a[...]=g_ref[...]
    factor(a,v,u,b)
    vh,vm,vl=split3(v[...]*1024.0)
    outs=[]
    for i in range(nch):
        loads[i].wait()
        xh,xm,xl=split3(xb[:,i*cw:(i+1)*cw])
        f=lambda p,q: jnp.dot(p,q,preferred_element_type=F32)
        acc=(f(vl,xh)+f(vh,xl)+f(vm,xm))+(f(vh,xm)+f(vm,xh))+f(vh,xh)
        ob[:,i*cw:(i+1)*cw]=acc
        c=pltpu.make_async_copy(ob.at[:,pl.ds(i*cw,cw)],o_hbm.at[:,pl.ds(i*cw,cw)],os.at[i]); c.start(); outs.append(c)
    ur=pltpu.roll(u[...],lax.rem(256-4*w,256),1)
    r_ref[...]=ur[:,0:4]*(1.0/1024.0)
    for c in outs: c.wait()

def finish(gram,x,b=64,cw=512):
    n,cells=x.shape
    return pl.pallas_call(functools.partial(finish_kernel,b,cw,0),
        out_shape=(jax.ShapeDtypeStruct((n,cells),F32),jax.ShapeDtypeStruct((n,4),F32)),
        in_specs=[pl.BlockSpec(memory_space=pltpu.VMEM),pl.BlockSpec(memory_space=pl.ANY)],
        out_specs=(pl.BlockSpec(memory_space=pl.ANY),pl.BlockSpec(memory_space=pltpu.VMEM)),
        scratch_shapes=[pltpu.VMEM((n,n),F32)]*3+[pltpu.VMEM((n,cells),F32)]*2+[pltpu.SemaphoreType.DMA((cells//cw,))]*2,
        compiler_params=pltpu.CompilerParams(vmem_limit_bytes=40<<20))(gram,x)


def to_peer(src, dst, send_sem, recv_sem, g, w):
    return pltpu.make_async_remote_copy(
        src_ref=src, dst_ref=dst, send_sem=send_sem, recv_sem=recv_sem, device_id=(g, w), device_id_type=MESH
    )


def wait_bytes(ref, sem):
    pltpu.make_async_copy(ref, ref, sem).wait()


def regroup_kernel(chunks, x_hbm, cells_hbm, gram_ref, buf, local, pieces, groups, total, send, recv, small, save):
    g, w = lax.axis_index("grp"), lax.axis_index("wr")
    snaps, own = buf.shape
    width = own // chunks
    rows = x_hbm.shape[0]
    writers = snaps // rows

    barrier = pltpu.get_barrier_semaphore()

    def greet(o, carry):
        pl.semaphore_signal(barrier, inc=1, device_id=(g, w ^ o), device_id_type=MESH)
        return carry

    lax.fori_loop(1, writers, greet, 0)
    for o in range(1, 4):
        pl.semaphore_signal(barrier, inc=1, device_id=(g ^ o, w), device_id_type=MESH)
    pl.semaphore_wait(barrier, writers - 1 + 3)

    mine = pl.ds(pl.multiple_of(w * rows, rows), rows)
    for c in range(chunks):

        def send_one(i, carry, c=c):
            p = w ^ lax.rem(i * 37 + w * 13 + c * 11, writers)
            src = x_hbm.at[:, pl.ds(pl.multiple_of(p * own + c * width, 128), width)]
            dst = buf.at[mine, pl.ds(c * width, width)]

            @pl.when(p == w)
            def _():
                pltpu.make_async_copy(src, dst, recv.at[c]).start()

            @pl.when(p != w)
            def _():
                to_peer(src, dst, send.at[0], recv.at[c], g, p).start()

            return carry

        lax.fori_loop(0, writers, send_one, 0)

    for c in range(chunks):
        part = buf.at[:, pl.ds(c * width, width)]
        wait_bytes(part, recv.at[c])
        pltpu.make_async_copy(part, cells_hbm.at[:, pl.ds(c * width, width)], save.at[c]).start()
        hi, mid, lo = split3(part[...])
        dot = lambda p, q: lax.dot_general(p, q, (((1,), (1,)), ((), ())), preferred_element_type=F32)
        cross = dot(hi, mid) + dot(hi, lo)
        term = (cross + cross.T) + dot(mid, mid) + dot(hi, hi)
        if c == 0:
            local[...] = term
        else:
            local[...] += term

    def scatter(o, carry):
        p = w ^ o
        to_peer(local.at[pl.ds(pl.multiple_of(p * rows, rows), rows), :], pieces.at[w], send.at[1], small.at[0], g, p).start()
        return carry

    pltpu.make_async_copy(local.at[mine, :], pieces.at[w], small.at[0]).start()
    lax.fori_loop(1, writers, scatter, 0)
    wait_bytes(pieces, small.at[0])
    groups[g] = jnp.sum(pieces[...], axis=0)
    for o in range(1, 4):
        to_peer(groups.at[g], groups.at[g], send.at[2], small.at[1], g ^ o, w).start()
    wait_bytes(groups.at[pl.ds(0, 3)], small.at[1])
    total[...] = (groups[0] + groups[1]) + (groups[2] + groups[3])

    def spread(o, carry):
        to_peer(total, gram_ref.at[mine, :], send.at[3], small.at[2], g, w ^ o).start()
        return carry

    pltpu.make_async_copy(total, gram_ref.at[mine, :], small.at[2]).start()
    lax.fori_loop(1, writers, spread, 0)
    wait_bytes(gram_ref, small.at[2])
    wait_bytes(x_hbm.at[:, pl.ds(0, (writers - 1) * own)], send.at[0])
    wait_bytes(pieces.at[pl.ds(0, writers - 1)], send.at[1])
    wait_bytes(groups.at[pl.ds(0, 3)], send.at[2])
    wait_bytes(pieces.at[pl.ds(0, writers - 1)], send.at[3])
    for c in range(chunks):
        wait_bytes(buf.at[:, pl.ds(c * width, width)], save.at[c])


def regroup(x, chunks=4):
    rows, cells = x.shape
    writers = lax.axis_size("wr")
    snaps, own = rows * writers, cells // writers
    return pl.pallas_call(
        functools.partial(regroup_kernel, chunks),
        out_shape=(jax.ShapeDtypeStruct((snaps, own), F32), jax.ShapeDtypeStruct((snaps, snaps), F32)),
        in_specs=[pl.BlockSpec(memory_space=pl.ANY)],
        out_specs=(pl.BlockSpec(memory_space=pl.ANY), pl.BlockSpec(memory_space=pltpu.VMEM)),
        scratch_shapes=[
            pltpu.VMEM((snaps, own), F32),
            pltpu.VMEM((snaps, snaps), F32),
            pltpu.VMEM((writers, rows, snaps), F32),
            pltpu.VMEM((4, rows, snaps), F32),
            pltpu.VMEM((rows, snaps), F32),
            pltpu.SemaphoreType.DMA((4,)),
            pltpu.SemaphoreType.DMA((chunks,)),
            pltpu.SemaphoreType.DMA((3,)),
            pltpu.SemaphoreType.DMA((chunks,)),
        ],
        compiler_params=pltpu.CompilerParams(
            collective_id=0, has_side_effects=True, vmem_limit_bytes=40 << 20
        ),
    )(x)


def body(snapshots):
    cells, gram = regroup(snapshots)
    return finish(gram, cells)


def solution(mesh):
    return jax.shard_map(
        body,
        mesh=mesh,
        in_specs=(P("wr", "grp"),),
        out_specs=(P(None, ("grp", "wr")), P(None, "wr")),
        check_vma=False,
    )
```

```python
import functools

import jax
import jax.numpy as jnp
from jax import lax
from jax.experimental import pallas as pl
from jax.experimental.pallas import tpu as pltpu
from jax.sharding import PartitionSpec as P

F32 = jnp.float32
BF = jnp.bfloat16
MESH = pl.DeviceIdType.MESH

CHUNKS = ((0, 3072), (3072, 1024))

def split3(v):
    hi=v.astype(BF); r=v-hi.astype(F32); mid=r.astype(BF); lo=(r-mid.astype(F32)).astype(BF)
    return hi,mid,lo

def rsqrt_exact(d):
    y=lax.rsqrt(d)
    return y*(1.5-0.5*d*y*y)

def factor(a_ref, v_ref, u_ref, b):
    n=a_ref.shape[0]; halves=n//128; groups=b//8
    lane=lax.broadcasted_iota(jnp.int32,(8,128),1); row=lax.broadcasted_iota(jnp.int32,(8,128),0)
    lane_all=lax.broadcasted_iota(jnp.int32,(n,n),1)
    lane_b=lax.broadcasted_iota(jnp.int32,(b,n),1); row_b=lax.broadcasted_iota(jnp.int32,(b,n),0)
    def panel(p,carry):
        k=pl.multiple_of(p*b,b)
        P=pltpu.roll(a_ref[pl.ds(k,b),:],lax.rem(n-k,n),1)
        G=[[P[8*g:8*g+8,128*h:128*h+128] for h in range(halves)] for g in range(groups)]
        UD=[None]*groups
        for q in range(groups):
            W=[{g:jnp.broadcast_to(G[g][0][:,8*q+j:8*q+j+1],(8,128)) for g in range(q,groups)} for j in range(8)]
            own=(lane>=8*q)&(lane<8*q+8)
            for g in range(q,groups):
                G[g][0]=jnp.where(own,(jnp.where(lane==row+8*q,1.0,0.0) if g==q else 0.0),G[g][0])
            dv=jnp.ones((8,128),F32)
            for j in range(8):
                d=W[j][q][j:j+1,:]
                r=1.0/d
                dv=jnp.where(row==j,d,dv)
                m={g:W[j][g]*r for g in range(q,groups)}
                m[q]=jnp.where(row>j,m[q],0.0)
                for jj in range(j+1,8):
                    pv=W[jj][q][j:j+1,:]
                    for g in range(q,groups): W[jj][g]=W[jj][g]-m[g]*pv
                pr=[G[q][h][j:j+1,:] for h in range(halves)]
                for g in range(q,groups):
                    for h in range(halves): G[g][h]=G[g][h]-m[g]*pr[h]
            s=rsqrt_exact(dv)
            ud=jnp.zeros((8,128),F32)
            for j in range(8): ud=jnp.where((lane==8*q+j)&(row<=j),W[j][q],ud)
            UD[q]=ud*s
            for h in range(halves): G[q][h]=G[q][h]*s
        Pf=jnp.concatenate([jnp.concatenate(g,axis=1) for g in G],axis=0)
        Pn=pltpu.roll(Pf,k,1)
        h3,m3,l3=split3(jnp.where((lane_b>row_b+k)&(lane_b<k+b),0.0,Pn))
        A=jnp.concatenate([h3,h3,m3,h3,l3,m3],axis=0)
        B=jnp.concatenate([h3,m3,h3,l3,h3,m3],axis=0)
        upd=lax.dot_general(A,B,(((0,),(0,)),((),())),preferred_element_type=F32)
        inpan=(lane_all>=k)&(lane_all<k+b)
        a_ref[...]=jnp.where(inpan,0.0,a_ref[...])-upd
        blk=(row_b//8)*8
        v_ref[pl.ds(k,b),:]=jnp.where(lane_b<=row_b+k,Pn,0.0)
        UDp=jnp.concatenate([jnp.concatenate([UD[g]]+[jnp.zeros((8,128),F32)]*(halves-1),axis=1) for g in range(groups)],axis=0)
        UDn=pltpu.roll(UDp,k,1)
        u_ref[pl.ds(k,b),:]=jnp.where(lane_b>=blk+k+8,Pn,UDn)
        return carry
    lax.fori_loop(0,n//b,panel,0)

def finish_kernel(b, cw, g_ref, x_ref, o_hbm, r_ref, a, v, u, ob, out_sem):
    n, cells = x_ref.shape
    w = lax.axis_index("wr")
    a[...] = g_ref[...]
    factor(a, v, u, b)
    vh, vm, vl = split3(v[...] * 1024.0)
    outs = []
    for i in range(cells // cw):
        xh, xm, xl = split3(x_ref[:, i * cw : (i + 1) * cw])
        f = lambda p, q: jnp.dot(p, q, preferred_element_type=F32)
        acc = (f(vl, xh) + f(vh, xl) + f(vm, xm)) + (f(vh, xm) + f(vm, xh)) + f(vh, xh)
        ob[:, i * cw : (i + 1) * cw] = acc
        c = pltpu.make_async_copy(ob.at[:, pl.ds(i * cw, cw)], o_hbm.at[:, pl.ds(i * cw, cw)], out_sem.at[i])
        c.start()
        outs.append(c)
    turned = pltpu.roll(u[...], lax.rem(n - 4 * w, n), 1)
    r_ref[...] = turned[:, 0:128].T[0:4, :] * (1.0 / 1024.0)
    for c in outs:
        c.wait()


def finish(gram, x, b=64, cw=512):
    n, cells = x.shape
    return pl.pallas_call(
        functools.partial(finish_kernel, b, cw),
        out_shape=(jax.ShapeDtypeStruct((n, cells), F32), jax.ShapeDtypeStruct((4, n), F32)),
        in_specs=[pl.BlockSpec(memory_space=pltpu.VMEM), pl.BlockSpec(memory_space=pltpu.VMEM)],
        out_specs=(pl.BlockSpec(memory_space=pltpu.HBM), pl.BlockSpec(memory_space=pltpu.VMEM)),
        scratch_shapes=[pltpu.VMEM((n, n), F32)] * 3 + [pltpu.VMEM((n, cells), F32), pltpu.SemaphoreType.DMA((cells // cw,))],
        compiler_params=pltpu.CompilerParams(vmem_limit_bytes=40 << 20),
    )(gram, x)


def to_peer(src, dst, send_sem, recv_sem, peer):
    return pltpu.make_async_remote_copy(
        src_ref=src, dst_ref=dst, send_sem=send_sem, recv_sem=recv_sem, device_id=peer, device_id_type=MESH
    )


def wait_bytes(ref, sem):
    pltpu.make_async_copy(ref, ref, sem).wait()


ORDER = (
    (0, 3, 1, 1),
    (2, 1, 1, 0),
    (3, 3, 0, 0),
    (0, 1, 1, 0),
    (2, 3, 0, 0),
    (0, 2, 0, 0),
    (1, 0, 1, 1),
    (3, 1, 0, 0),
    (2, 2, 1, 0),
    (1, 0, 1, 0),
    (3, 2, 0, 0),
    (2, 2, 1, 1),
    (2, 3, 1, 0),
    (0, 1, 0, 0),
    (0, 0, 0, 1),
    (2, 3, 0, 1),
    (3, 3, 1, 0),
    (1, 1, 1, 1),
    (1, 2, 0, 0),
    (3, 0, 1, 1),
    (2, 2, 0, 0),
    (0, 1, 0, 1),
    (0, 3, 1, 0),
    (2, 0, 0, 0),
    (0, 0, 1, 0),
    (2, 1, 0, 1),
    (0, 3, 0, 0),
    (0, 1, 1, 1),
    (3, 3, 0, 1),
    (2, 0, 1, 1),
    (1, 2, 0, 1),
    (3, 2, 1, 0),
    (1, 1, 1, 0),
    (2, 3, 1, 1),
    (0, 2, 0, 1),
    (3, 0, 0, 1),
    (1, 3, 0, 0),
    (3, 1, 1, 0),
    (1, 0, 0, 0),
    (3, 1, 0, 1),
    (1, 3, 1, 0),
    (3, 2, 0, 1),
    (1, 2, 1, 1),
    (0, 0, 1, 1),
    (3, 0, 0, 0),
    (1, 3, 0, 1),
    (2, 1, 1, 1),
    (0, 2, 1, 1),
    (2, 1, 0, 0),
    (0, 3, 0, 1),
    (3, 0, 1, 0),
    (1, 3, 1, 1),
    (1, 1, 0, 0),
    (1, 2, 1, 0),
    (2, 2, 0, 1),
    (3, 3, 1, 1),
    (3, 1, 1, 1),
    (2, 0, 0, 1),
    (0, 2, 1, 0),
    (1, 0, 0, 1),
    (3, 2, 1, 1),
    (1, 1, 0, 1),
    (2, 0, 1, 0),
)
RING = tuple(range(1, 8))


def regroup_kernel(chunks, x_hbm, cells_ref, gram_ref, staged, local, other, half, pieces, layers, total, send, recv, small, load):
    g, w = lax.axis_index("grp"), lax.axis_index("wr")
    snaps, own = cells_ref.shape
    rows = x_hbm.shape[0]
    writers = snaps // rows
    core, zlo, place = lax.rem(w, 2), lax.rem(w // 2, 2), w // 4
    x, y = lax.rem(place, 4), place // 4

    pieces_in = 4
    span = x_hbm.shape[1] // pieces_in
    loads = [
        pltpu.make_async_copy(x_hbm.at[:, pl.ds(i * span, span)], staged.at[:, pl.ds(i * span, span)], load.at[i])
        for i in range(pieces_in)
    ]
    for copy in loads:
        copy.start()

    def peer(offset):
        dy, dx, dz, dc = offset
        at_y, at_x = lax.rem(y + dy, 4), lax.rem(x + dx, 4)
        return g, ((at_y * 4 + at_x) * 2 + lax.rem(zlo + dz, 2)) * 2 + lax.rem(core + dc, 2)

    def along_z(step):
        z = lax.rem(g * 2 + zlo + step, 8)
        return z // 2, w + 2 * (lax.rem(z, 2) - zlo)

    barrier = pltpu.get_barrier_semaphore()

    def greet(to):
        pl.semaphore_signal(barrier, inc=1, device_id=to, device_id_type=MESH)

    def greet_group(o, carry):
        greet((g, w ^ o))
        return carry

    def greet_ring(step, carry):
        to = along_z(step)

        @pl.when(to[0] != g)
        def _():
            greet(to)

        return carry

    lax.fori_loop(1, 8, greet_ring, 0)
    lax.fori_loop(1, writers, greet_group, 0)
    pl.semaphore_wait(barrier, writers - 1 + 6)
    for copy in loads:
        copy.wait()

    mine = pl.ds(pl.multiple_of(w * rows, rows), rows)
    for c, (first, width) in enumerate(chunks):
        at = pl.ds(first, width)

        def source(p):
            return staged.at[:, pl.ds(pl.multiple_of(p * own + first, 128), width)]

        for o in ORDER:
            to = peer(o)
            to_peer(source(to[1]), cells_ref.at[mine, at], send.at[0], recv.at[c], to).start()
        pltpu.make_async_copy(source(w), cells_ref.at[mine, at], recv.at[c]).start()

    dot = lambda p, q: lax.dot_general(p, q, (((1,), (1,)), ((), ())), preferred_element_type=F32)
    for c, (first, width) in enumerate(chunks):
        part = cells_ref.at[:, pl.ds(first, width)]
        wait_bytes(part, recv.at[c])
        hi, mid, lo = split3(part[...])
        small_terms = (dot(hi, lo) + dot(lo, hi) + dot(mid, mid)) + (dot(hi, mid) + dot(mid, hi))
        term = small_terms + dot(hi, hi)
        local[...] = term if c == 0 else local[...] + term

    deep = snaps // 2
    strip = deep // 16
    to_peer(
        local.at[pl.ds(pl.multiple_of((1 - core) * deep, deep), deep), :], other, send.at[1], small.at[0], (g, w ^ 1)
    ).start()
    wait_bytes(other, small.at[0])
    half[...] = local[pl.ds(pl.multiple_of(core * deep, deep), deep), :] + other[...]

    def strip_of(p):
        return pl.ds(pl.multiple_of(p * strip, strip), strip)

    def scatter(o, carry):
        p = place ^ o
        to_peer(half.at[strip_of(p), :], pieces.at[place], send.at[2], small.at[1], (g, w ^ (4 * o))).start()
        return carry

    lax.fori_loop(1, 16, scatter, 0)
    pieces[place] = half[strip_of(place), :]
    wait_bytes(pieces.at[pl.ds(0, 15)], small.at[1])
    layer = g * 2 + zlo
    layers[layer] = jnp.sum(pieces[...], axis=0)
    for step in RING:
        to_peer(layers.at[layer], layers.at[layer], send.at[3], small.at[2], along_z(step)).start()
    wait_bytes(layers.at[pl.ds(0, 7)], small.at[2])
    total[...] = jnp.sum(layers[...], axis=0)
    rows_out = pl.ds(pl.multiple_of(core * deep + place * strip, strip), strip)

    def spread(o, carry):
        to_peer(total, gram_ref.at[rows_out, :], send.at[4], small.at[3], (g, w ^ (4 * (o // 2) + lax.rem(o, 2)))).start()
        return carry

    lax.fori_loop(1, 32, spread, 0)
    gram_ref[rows_out, :] = total[...]
    wait_bytes(gram_ref.at[pl.ds(0, 31 * strip), :], small.at[3])
    wait_bytes(staged.at[:, pl.ds(0, (writers - 1) * own)], send.at[0])
    wait_bytes(other, send.at[1])
    wait_bytes(pieces.at[pl.ds(0, 15)], send.at[2])
    wait_bytes(layers.at[pl.ds(0, 7)], send.at[3])
    wait_bytes(gram_ref.at[pl.ds(0, 31 * strip), :], send.at[4])


def regroup(x):
    rows, cells = x.shape
    writers = lax.axis_size("wr")
    snaps, own = rows * writers, cells // writers
    chunks = CHUNKS
    return pl.pallas_call(
        functools.partial(regroup_kernel, chunks),
        out_shape=(jax.ShapeDtypeStruct((snaps, own), F32), jax.ShapeDtypeStruct((snaps, snaps), F32)),
        in_specs=[pl.BlockSpec(memory_space=pltpu.HBM)],
        out_specs=(pl.BlockSpec(memory_space=pltpu.VMEM), pl.BlockSpec(memory_space=pltpu.VMEM)),
        scratch_shapes=[
            pltpu.VMEM((rows, cells), F32),
            pltpu.VMEM((snaps, snaps), F32),
            pltpu.VMEM((snaps // 2, snaps), F32),
            pltpu.VMEM((snaps // 2, snaps), F32),
            pltpu.VMEM((16, snaps // 32, snaps), F32),
            pltpu.VMEM((8, snaps // 32, snaps), F32),
            pltpu.VMEM((snaps // 32, snaps), F32),
            pltpu.SemaphoreType.DMA((5,)),
            pltpu.SemaphoreType.DMA((len(chunks),)),
            pltpu.SemaphoreType.DMA((4,)),
            pltpu.SemaphoreType.DMA((4,)),
        ],
        compiler_params=pltpu.CompilerParams(
            collective_id=0, has_side_effects=True, vmem_limit_bytes=48 << 20
        ),
    )(x)


def body(snapshots):
    cells, gram = regroup(snapshots)
    basis, columns = finish(gram, cells)
    return basis, columns.T


def solution(mesh):
    return jax.shard_map(
        body,
        mesh=mesh,
        in_specs=(P("wr", "grp"),),
        out_specs=(P(None, ("grp", "wr")), P(None, "wr")),
        check_vma=False,
    )
```

```python
import functools

import jax
import jax.numpy as jnp
from jax import lax
from jax.experimental import pallas as pl
from jax.experimental.pallas import tpu as pltpu
from jax.sharding import PartitionSpec as P

F32 = jnp.float32
BF = jnp.bfloat16
MESH = pl.DeviceIdType.MESH

CHUNKS = ((0, 3072), (3072, 1024))

def split3(v):
    hi=v.astype(BF); r=v-hi.astype(F32); mid=r.astype(BF); lo=(r-mid.astype(F32)).astype(BF)
    return hi,mid,lo

def rsqrt_exact(d):
    y=lax.rsqrt(d)
    return y*(1.5-0.5*d*y*y)

def pick(rows, l):
    where = jnp.full(rows.shape, l, jnp.int32)
    return jnp.take_along_axis(rows, where, axis=1, mode="promise_in_bounds")


def factor(a_ref, v_ref, u_ref, b, product, rows_out):
    n=a_ref.shape[0]; halves=n//128; groups=b//8
    lane=lax.broadcasted_iota(jnp.int32,(8,128),1); row=lax.broadcasted_iota(jnp.int32,(8,128),0)
    lane_all=lax.broadcasted_iota(jnp.int32,(n,n),1)
    lane_b=lax.broadcasted_iota(jnp.int32,(b,n),1); row_b=lax.broadcasted_iota(jnp.int32,(b,n),0)
    def panel(p,carry):
        k=pl.multiple_of(p*b,b)
        product(jnp.maximum(p-1,0))
        P=pltpu.roll(a_ref[pl.ds(k,b),:],lax.rem(n-k,n),1)
        G=[[P[8*g:8*g+8,128*h:128*h+128] for h in range(halves)] for g in range(groups)]
        UD=[None]*groups
        for q in range(groups):
            W=[{g:pick(G[g][0],8*q+j) for g in range(q+(q>0),groups)} for j in range(8)]
            if q>0:
                for j in range(8): W[j][q]=ahead[j]
            if q+1<groups: ahead=[pick(G[q+1][0],8*q+8+j) for j in range(8)]
            own=(lane>=8*q)&(lane<8*q+8)
            for g in range(q,groups):
                G[g][0]=jnp.where(own,(jnp.where(lane==row+8*q,1.0,0.0) if g==q else 0.0),G[g][0])
            dv=jnp.ones((8,128),F32)
            for j in range(8):
                d=W[j][q][j:j+1,:]
                r=1.0/d
                dv=jnp.where(row==j,d,dv)
                m={g:W[j][g]*r for g in range(q,groups)}
                m[q]=jnp.where(row>j,m[q],0.0)
                for jj in range(j+1,8):
                    pv=W[jj][q][j:j+1,:]
                    for g in range(q,groups): W[jj][g]=W[jj][g]-m[g]*pv
                if q+1<groups:
                    for jj in range(8): ahead[jj]=ahead[jj]-m[q+1]*W[j][q+1][jj:jj+1,:]
                pr=[G[q][h][j:j+1,:] for h in range(halves)]
                for g in range(q,groups):
                    for h in range(halves): G[g][h]=G[g][h]-m[g]*pr[h]
            s=rsqrt_exact(dv)
            ud=jnp.zeros((8,128),F32)
            for j in range(8): ud=jnp.where((lane==8*q+j)&(row<=j),W[j][q],ud)
            UD[q]=ud*s
            for h in range(halves): G[q][h]=G[q][h]*s
        Pf=jnp.concatenate([jnp.concatenate(g,axis=1) for g in G],axis=0)
        Pn=pltpu.roll(Pf,k,1)
        h3,m3,l3=split3(jnp.where((lane_b>row_b+k)&(lane_b<k+b),0.0,Pn))
        A=jnp.concatenate([h3,h3,m3,h3,l3,m3],axis=0)
        B=jnp.concatenate([h3,m3,h3,l3,h3,m3],axis=0)
        upd=lax.dot_general(A,B,(((0,),(0,)),((),())),preferred_element_type=F32)
        inpan=(lane_all>=k)&(lane_all<k+b)
        a_ref[...]=jnp.where(inpan,0.0,a_ref[...])-upd
        blk=(row_b//8)*8
        v_ref[pl.ds(k,b),:]=jnp.where(lane_b<=row_b+k,Pn,0.0)
        UDp=jnp.concatenate([jnp.concatenate([UD[g]]+[jnp.zeros((8,128),F32)]*(halves-1),axis=1) for g in range(groups)],axis=0)
        UDn=pltpu.roll(UDp,k,1)
        u_ref[pl.ds(k,b),:]=jnp.where(lane_b>=blk+k+8,Pn,UDn)
        @pl.when(p>0)
        def _(): rows_out(p-1).start()
        return carry
    lax.fori_loop(0,n//b,panel,0)
    product(n//b-1)
    rows_out(n//b-1).start()

def finish_kernel(b, cw, g_ref, xh_ref, xm_ref, xl_ref, o_hbm, r_ref, a, v, u, ob, out_sem):
    n, cells = xh_ref.shape
    w = lax.axis_index("wr")
    a[...] = g_ref[...]
    v[0:b, :] = jnp.zeros((b, n), F32)

    def product(p):
        at = pl.ds(pl.multiple_of(p * b, b), b)
        vh, vm, vl = split3(v[at, :] * 1024.0)
        three, two = jnp.concatenate([vh, vm, vl], axis=0), jnp.concatenate([vh, vm], axis=0)
        f = lambda l, r: jnp.dot(l, r, preferred_element_type=F32)
        for i in range(cells // cw):
            part = slice(i * cw, (i + 1) * cw)
            th, tm, tl = f(three, xh_ref[:, part]), f(two, xm_ref[:, part]), f(vh, xl_ref[:, part])
            ob[at, part] = (th[2 * b :] + tm[b:] + tl) + (th[b : 2 * b] + tm[:b]) + th[:b]

    def rows_out(p):
        at = pl.ds(pl.multiple_of(p * b, b), b)
        return pltpu.make_async_copy(ob.at[at, :], o_hbm.at[at, :], out_sem.at[p])

    factor(a, v, u, b, product, rows_out)
    turned = pltpu.roll(u[...], lax.rem(n - 4 * w, n), 1)
    r_ref[...] = turned[:, 0:128].T[0:4, :] * (1.0 / 1024.0)
    for p in range(n // b):
        rows_out(p).wait()


def finish(gram, x, b=64, cw=512):
    n, cells = x[0].shape
    return pl.pallas_call(
        functools.partial(finish_kernel, b, cw),
        out_shape=(jax.ShapeDtypeStruct((n, cells), F32), jax.ShapeDtypeStruct((4, n), F32)),
        in_specs=[pl.BlockSpec(memory_space=pltpu.VMEM)] * 4,
        out_specs=(pl.BlockSpec(memory_space=pltpu.HBM), pl.BlockSpec(memory_space=pltpu.VMEM)),
        scratch_shapes=[pltpu.VMEM((n, n), F32)] * 3 + [pltpu.VMEM((n, cells), F32), pltpu.SemaphoreType.DMA((n // b,))],
        compiler_params=pltpu.CompilerParams(vmem_limit_bytes=40 << 20),
    )(gram, *x)


def to_peer(src, dst, send_sem, recv_sem, peer):
    return pltpu.make_async_remote_copy(
        src_ref=src, dst_ref=dst, send_sem=send_sem, recv_sem=recv_sem, device_id=peer, device_id_type=MESH
    )


def wait_bytes(ref, sem):
    pltpu.make_async_copy(ref, ref, sem).wait()


ORDER = (
    (0, 3, 1, 1),
    (2, 1, 1, 0),
    (3, 3, 0, 0),
    (0, 1, 1, 0),
    (2, 3, 0, 0),
    (0, 2, 0, 0),
    (1, 0, 1, 1),
    (3, 1, 0, 0),
    (2, 2, 1, 0),
    (1, 0, 1, 0),
    (3, 2, 0, 0),
    (2, 2, 1, 1),
    (2, 3, 1, 0),
    (0, 1, 0, 0),
    (0, 0, 0, 1),
    (2, 3, 0, 1),
    (3, 3, 1, 0),
    (1, 1, 1, 1),
    (1, 2, 0, 0),
    (3, 0, 1, 1),
    (2, 2, 0, 0),
    (0, 1, 0, 1),
    (0, 3, 1, 0),
    (2, 0, 0, 0),
    (0, 0, 1, 0),
    (2, 1, 0, 1),
    (0, 3, 0, 0),
    (0, 1, 1, 1),
    (3, 3, 0, 1),
    (2, 0, 1, 1),
    (1, 2, 0, 1),
    (3, 2, 1, 0),
    (1, 1, 1, 0),
    (2, 3, 1, 1),
    (0, 2, 0, 1),
    (3, 0, 0, 1),
    (1, 3, 0, 0),
    (3, 1, 1, 0),
    (1, 0, 0, 0),
    (3, 1, 0, 1),
    (1, 3, 1, 0),
    (3, 2, 0, 1),
    (1, 2, 1, 1),
    (0, 0, 1, 1),
    (3, 0, 0, 0),
    (1, 3, 0, 1),
    (2, 1, 1, 1),
    (0, 2, 1, 1),
    (2, 1, 0, 0),
    (0, 3, 0, 1),
    (3, 0, 1, 0),
    (1, 3, 1, 1),
    (1, 1, 0, 0),
    (1, 2, 1, 0),
    (2, 2, 0, 1),
    (3, 3, 1, 1),
    (3, 1, 1, 1),
    (2, 0, 0, 1),
    (0, 2, 1, 0),
    (1, 0, 0, 1),
    (3, 2, 1, 1),
    (1, 1, 0, 1),
    (2, 0, 1, 0),
)
RING = tuple(range(1, 8))


def regroup_kernel(chunks, x_hbm, high_ref, mid_ref, low_ref, gram_ref, cells_ref, staged, local, other, half, pieces, layers, total, send, recv, small, load):
    g, w = lax.axis_index("grp"), lax.axis_index("wr")
    snaps, own = cells_ref.shape
    rows = x_hbm.shape[0]
    writers = snaps // rows
    core, zlo, place = lax.rem(w, 2), lax.rem(w // 2, 2), w // 4
    x, y = lax.rem(place, 4), place // 4

    pieces_in = 4
    span = x_hbm.shape[1] // pieces_in
    loads = [
        pltpu.make_async_copy(x_hbm.at[:, pl.ds(i * span, span)], staged.at[:, pl.ds(i * span, span)], load.at[i])
        for i in range(pieces_in)
    ]
    for copy in loads:
        copy.start()

    def peer(offset):
        dy, dx, dz, dc = offset
        at_y, at_x = lax.rem(y + dy, 4), lax.rem(x + dx, 4)
        return g, ((at_y * 4 + at_x) * 2 + lax.rem(zlo + dz, 2)) * 2 + lax.rem(core + dc, 2)

    def along_z(step):
        z = lax.rem(g * 2 + zlo + step, 8)
        return z // 2, w + 2 * (lax.rem(z, 2) - zlo)

    barrier = pltpu.get_barrier_semaphore()

    def greet(to):
        pl.semaphore_signal(barrier, inc=1, device_id=to, device_id_type=MESH)

    def greet_group(o, carry):
        greet((g, w ^ o))
        return carry

    def greet_ring(step, carry):
        to = along_z(step)

        @pl.when(to[0] != g)
        def _():
            greet(to)

        return carry

    lax.fori_loop(1, 8, greet_ring, 0)
    lax.fori_loop(1, writers, greet_group, 0)
    pl.semaphore_wait(barrier, writers - 1 + 6)
    for copy in loads:
        copy.wait()

    mine = pl.ds(pl.multiple_of(w * rows, rows), rows)
    for c, (first, width) in enumerate(chunks):
        at = pl.ds(first, width)

        def source(p):
            return staged.at[:, pl.ds(pl.multiple_of(p * own + first, 128), width)]

        for o in ORDER:
            to = peer(o)
            to_peer(source(to[1]), cells_ref.at[mine, at], send.at[0], recv.at[c], to).start()
        pltpu.make_async_copy(source(w), cells_ref.at[mine, at], recv.at[c]).start()

    dot = lambda p, q: lax.dot_general(p, q, (((1,), (1,)), ((), ())), preferred_element_type=F32)
    for c, (first, width) in enumerate(chunks):
        part = cells_ref.at[:, pl.ds(first, width)]
        wait_bytes(part, recv.at[c])
        hi, mid, lo = split3(part[...])
        at = pl.ds(first, width)
        high_ref[:, at], mid_ref[:, at], low_ref[:, at] = hi, mid, lo
        small_terms = (dot(hi, lo) + dot(lo, hi) + dot(mid, mid)) + (dot(hi, mid) + dot(mid, hi))
        term = small_terms + dot(hi, hi)
        local[...] = term if c == 0 else local[...] + term

    deep = snaps // 2
    strip = deep // 16
    to_peer(
        local.at[pl.ds(pl.multiple_of((1 - core) * deep, deep), deep), :], other, send.at[1], small.at[0], (g, w ^ 1)
    ).start()
    wait_bytes(other, small.at[0])
    half[...] = local[pl.ds(pl.multiple_of(core * deep, deep), deep), :] + other[...]

    def strip_of(p):
        return pl.ds(pl.multiple_of(p * strip, strip), strip)

    def scatter(o, carry):
        p = place ^ o
        to_peer(half.at[strip_of(p), :], pieces.at[place], send.at[2], small.at[1], (g, w ^ (4 * o))).start()
        return carry

    lax.fori_loop(1, 16, scatter, 0)
    pieces[place] = half[strip_of(place), :]
    wait_bytes(pieces.at[pl.ds(0, 15)], small.at[1])
    layer = g * 2 + zlo
    layers[layer] = jnp.sum(pieces[...], axis=0)
    for step in RING:
        to_peer(layers.at[layer], layers.at[layer], send.at[3], small.at[2], along_z(step)).start()
    wait_bytes(layers.at[pl.ds(0, 7)], small.at[2])
    total[...] = jnp.sum(layers[...], axis=0)
    rows_out = pl.ds(pl.multiple_of(core * deep + place * strip, strip), strip)

    def spread(o, carry):
        to_peer(total, gram_ref.at[rows_out, :], send.at[4], small.at[3], (g, w ^ (4 * (o // 2) + lax.rem(o, 2)))).start()
        return carry

    lax.fori_loop(1, 32, spread, 0)
    gram_ref[rows_out, :] = total[...]
    wait_bytes(gram_ref.at[pl.ds(0, 31 * strip), :], small.at[3])
    wait_bytes(staged.at[:, pl.ds(0, (writers - 1) * own)], send.at[0])
    wait_bytes(other, send.at[1])
    wait_bytes(pieces.at[pl.ds(0, 15)], send.at[2])
    wait_bytes(layers.at[pl.ds(0, 7)], send.at[3])
    wait_bytes(gram_ref.at[pl.ds(0, 31 * strip), :], send.at[4])


def regroup(x):
    rows, cells = x.shape
    writers = lax.axis_size("wr")
    snaps, own = rows * writers, cells // writers
    chunks = CHUNKS
    return pl.pallas_call(
        functools.partial(regroup_kernel, chunks),
        out_shape=(*[jax.ShapeDtypeStruct((snaps, own), BF)] * 3, jax.ShapeDtypeStruct((snaps, snaps), F32)),
        in_specs=[pl.BlockSpec(memory_space=pltpu.HBM)],
        out_specs=(pl.BlockSpec(memory_space=pltpu.VMEM),) * 4,
        scratch_shapes=[
            pltpu.VMEM((snaps, own), F32),
            pltpu.VMEM((rows, cells), F32),
            pltpu.VMEM((snaps, snaps), F32),
            pltpu.VMEM((snaps // 2, snaps), F32),
            pltpu.VMEM((snaps // 2, snaps), F32),
            pltpu.VMEM((16, snaps // 32, snaps), F32),
            pltpu.VMEM((8, snaps // 32, snaps), F32),
            pltpu.VMEM((snaps // 32, snaps), F32),
            pltpu.SemaphoreType.DMA((5,)),
            pltpu.SemaphoreType.DMA((len(chunks),)),
            pltpu.SemaphoreType.DMA((4,)),
            pltpu.SemaphoreType.DMA((4,)),
        ],
        compiler_params=pltpu.CompilerParams(
            collective_id=0, has_side_effects=True, vmem_limit_bytes=46 << 20
        ),
    )(x)


def body(snapshots):
    *cells, gram = regroup(snapshots)
    basis, columns = finish(gram, cells)
    return basis, columns.T


def solution(mesh):
    return jax.shard_map(
        body,
        mesh=mesh,
        in_specs=(P("wr", "grp"),),
        out_specs=(P(None, ("grp", "wr")), P(None, "wr")),
        check_vma=False,
    )
```

```python
import functools

import jax
import jax.numpy as jnp
from jax import lax
from jax.experimental import pallas as pl
from jax.experimental.pallas import tpu as pltpu
from jax.sharding import PartitionSpec as P

F32 = jnp.float32
BF = jnp.bfloat16
MESH = pl.DeviceIdType.MESH

CHUNKS = ((0, 2560), (2560, 1024), (3584, 512))

def split3(v):
    hi=v.astype(BF); r=v-hi.astype(F32); mid=r.astype(BF); lo=(r-mid.astype(F32)).astype(BF)
    return hi,mid,lo

def rsqrt_exact(d):
    y=lax.rsqrt(d)
    return y*(1.5-0.5*d*y*y)

def pick(rows, l):
    where = jnp.full(rows.shape, l, jnp.int32)
    return jnp.take_along_axis(rows, where, axis=1, mode="promise_in_bounds")


def factor(a_ref, v_ref, u_ref, b, product, rows_out):
    n=a_ref.shape[0]; halves=n//128; groups=b//8
    lane=lax.broadcasted_iota(jnp.int32,(8,128),1); row=lax.broadcasted_iota(jnp.int32,(8,128),0)
    lane_all=lax.broadcasted_iota(jnp.int32,(n,n),1)
    lane_b=lax.broadcasted_iota(jnp.int32,(b,n),1); row_b=lax.broadcasted_iota(jnp.int32,(b,n),0)
    def panel(p,carry):
        k=pl.multiple_of(p*b,b)
        product(jnp.maximum(p-1,0))
        P=pltpu.roll(a_ref[pl.ds(k,b),:],lax.rem(n-k,n),1)
        G=[[P[8*g:8*g+8,128*h:128*h+128] for h in range(halves)] for g in range(groups)]
        UD=[None]*groups
        for q in range(groups):
            W=[{g:pick(G[g][0],8*q+j) for g in range(q+(q>0),groups)} for j in range(8)]
            if q>0:
                for j in range(8): W[j][q]=ahead[j]
            if q+1<groups: ahead=[pick(G[q+1][0],8*q+8+j) for j in range(8)]
            own=(lane>=8*q)&(lane<8*q+8)
            for g in range(q,groups):
                G[g][0]=jnp.where(own,(jnp.where(lane==row+8*q,1.0,0.0) if g==q else 0.0),G[g][0])
            dv=jnp.ones((8,128),F32)
            for j in range(8):
                d=W[j][q][j:j+1,:]
                r=1.0/d
                dv=jnp.where(row==j,d,dv)
                m={g:W[j][g]*r for g in range(q,groups)}
                m[q]=jnp.where(row>j,m[q],0.0)
                for jj in range(j+1,8):
                    pv=W[jj][q][j:j+1,:]
                    for g in range(q,groups): W[jj][g]=W[jj][g]-m[g]*pv
                if q+1<groups:
                    for jj in range(8): ahead[jj]=ahead[jj]-m[q+1]*W[j][q+1][jj:jj+1,:]
                pr=[G[q][h][j:j+1,:] for h in range(halves)]
                for g in range(q,groups):
                    for h in range(halves): G[g][h]=G[g][h]-m[g]*pr[h]
            s=rsqrt_exact(dv)
            ud=jnp.zeros((8,128),F32)
            for j in range(8): ud=jnp.where((lane==8*q+j)&(row<=j),W[j][q],ud)
            UD[q]=ud*s
            for h in range(halves): G[q][h]=G[q][h]*s
        Pf=jnp.concatenate([jnp.concatenate(g,axis=1) for g in G],axis=0)
        Pn=pltpu.roll(Pf,k,1)
        h3,m3,l3=split3(jnp.where((lane_b>row_b+k)&(lane_b<k+b),0.0,Pn))
        A=jnp.concatenate([h3,h3,m3,h3,l3,m3],axis=0)
        B=jnp.concatenate([h3,m3,h3,l3,h3,m3],axis=0)
        upd=lax.dot_general(A,B,(((0,),(0,)),((),())),preferred_element_type=F32)
        inpan=(lane_all>=k)&(lane_all<k+b)
        a_ref[...]=jnp.where(inpan,0.0,a_ref[...])-upd
        blk=(row_b//8)*8
        v_ref[pl.ds(k,b),:]=jnp.where(lane_b<=row_b+k,Pn,0.0)
        UDp=jnp.concatenate([jnp.concatenate([UD[g]]+[jnp.zeros((8,128),F32)]*(halves-1),axis=1) for g in range(groups)],axis=0)
        UDn=pltpu.roll(UDp,k,1)
        u_ref[pl.ds(k,b),:]=jnp.where(lane_b>=blk+k+8,Pn,UDn)
        @pl.when(p>0)
        def _(): rows_out(p-1).start()
        return carry
    lax.fori_loop(0,n//b,panel,0)
    product(n//b-1)
    rows_out(n//b-1).start()

def finish_kernel(b, cw, g_ref, xh_ref, xm_ref, xl_ref, o_hbm, r_ref, a, v, u, ob, out_sem):
    n, cells = xh_ref.shape
    w = lax.axis_index("wr")
    a[...] = g_ref[...]
    v[0:b, :] = jnp.zeros((b, n), F32)

    def product(p):
        at = pl.ds(pl.multiple_of(p * b, b), b)
        vh, vm, vl = split3(v[at, :] * 1024.0)
        three, two = jnp.concatenate([vh, vm, vl], axis=0), jnp.concatenate([vh, vm], axis=0)
        f = lambda l, r: jnp.dot(l, r, preferred_element_type=F32)
        for i in range(cells // cw):
            part = slice(i * cw, (i + 1) * cw)
            th, tm, tl = f(three, xh_ref[:, part]), f(two, xm_ref[:, part]), f(vh, xl_ref[:, part])
            ob[at, part] = (th[2 * b :] + tm[b:] + tl) + (th[b : 2 * b] + tm[:b]) + th[:b]

    def rows_out(p):
        at = pl.ds(pl.multiple_of(p * b, b), b)
        return pltpu.make_async_copy(ob.at[at, :], o_hbm.at[at, :], out_sem.at[p])

    factor(a, v, u, b, product, rows_out)
    turned = pltpu.roll(u[...], lax.rem(n - 4 * w, n), 1)
    r_ref[...] = turned[:, 0:128].T[0:4, :] * (1.0 / 1024.0)
    for p in range(n // b):
        rows_out(p).wait()


def finish(gram, x, b=64, cw=512):
    n, cells = x[0].shape
    return pl.pallas_call(
        functools.partial(finish_kernel, b, cw),
        out_shape=(jax.ShapeDtypeStruct((n, cells), F32), jax.ShapeDtypeStruct((4, n), F32)),
        in_specs=[pl.BlockSpec(memory_space=pltpu.VMEM)] * 4,
        out_specs=(pl.BlockSpec(memory_space=pltpu.HBM), pl.BlockSpec(memory_space=pltpu.VMEM)),
        scratch_shapes=[pltpu.VMEM((n, n), F32)] * 3 + [pltpu.VMEM((n, cells), F32), pltpu.SemaphoreType.DMA((n // b,))],
        compiler_params=pltpu.CompilerParams(vmem_limit_bytes=40 << 20),
    )(gram, *x)


def to_peer(src, dst, send_sem, recv_sem, peer):
    return pltpu.make_async_remote_copy(
        src_ref=src, dst_ref=dst, send_sem=send_sem, recv_sem=recv_sem, device_id=peer, device_id_type=MESH
    )


def wait_bytes(ref, sem):
    pltpu.make_async_copy(ref, ref, sem).wait()


ORDER = (
    (0, 3, 1, 1),
    (2, 1, 1, 0),
    (3, 3, 0, 0),
    (0, 1, 1, 0),
    (2, 3, 0, 0),
    (0, 2, 0, 0),
    (1, 0, 1, 1),
    (3, 1, 0, 0),
    (2, 2, 1, 0),
    (1, 0, 1, 0),
    (3, 2, 0, 0),
    (2, 2, 1, 1),
    (2, 3, 1, 0),
    (0, 1, 0, 0),
    (0, 0, 0, 1),
    (2, 3, 0, 1),
    (3, 3, 1, 0),
    (1, 1, 1, 1),
    (1, 2, 0, 0),
    (3, 0, 1, 1),
    (2, 2, 0, 0),
    (0, 1, 0, 1),
    (0, 3, 1, 0),
    (2, 0, 0, 0),
    (0, 0, 1, 0),
    (2, 1, 0, 1),
    (0, 3, 0, 0),
    (0, 1, 1, 1),
    (3, 3, 0, 1),
    (2, 0, 1, 1),
    (1, 2, 0, 1),
    (3, 2, 1, 0),
    (1, 1, 1, 0),
    (2, 3, 1, 1),
    (0, 2, 0, 1),
    (3, 0, 0, 1),
    (1, 3, 0, 0),
    (3, 1, 1, 0),
    (1, 0, 0, 0),
    (3, 1, 0, 1),
    (1, 3, 1, 0),
    (3, 2, 0, 1),
    (1, 2, 1, 1),
    (0, 0, 1, 1),
    (3, 0, 0, 0),
    (1, 3, 0, 1),
    (2, 1, 1, 1),
    (0, 2, 1, 1),
    (2, 1, 0, 0),
    (0, 3, 0, 1),
    (3, 0, 1, 0),
    (1, 3, 1, 1),
    (1, 1, 0, 0),
    (1, 2, 1, 0),
    (2, 2, 0, 1),
    (3, 3, 1, 1),
    (3, 1, 1, 1),
    (2, 0, 0, 1),
    (0, 2, 1, 0),
    (1, 0, 0, 1),
    (3, 2, 1, 1),
    (1, 1, 0, 1),
    (2, 0, 1, 0),
)
RING = (4, 3, 5, 2, 6, 1, 7)
HOPS = (0, 1, 2, 1)
FAR_FIRST = sorted(range(1, 32), key=lambda o: -HOPS[o // 8] - HOPS[o // 2 % 4])


def regroup_kernel(chunks, x_hbm, high_ref, mid_ref, low_ref, gram_ref, cells_ref, staged, local, pieces, layers, total, send, recv, small, load):
    g, w = lax.axis_index("grp"), lax.axis_index("wr")
    snaps, own = cells_ref.shape
    rows = x_hbm.shape[0]
    writers = snaps // rows
    core, zlo, place = lax.rem(w, 2), lax.rem(w // 2, 2), w // 4
    x, y = lax.rem(place, 4), place // 4

    pieces_in = 4
    span = x_hbm.shape[1] // pieces_in
    loads = [
        pltpu.make_async_copy(x_hbm.at[:, pl.ds(i * span, span)], staged.at[:, pl.ds(i * span, span)], load.at[i])
        for i in range(pieces_in)
    ]
    for copy in loads:
        copy.start()

    def peer(offset):
        dy, dx, dz, dc = offset
        at_y, at_x = lax.rem(y + dy, 4), lax.rem(x + dx, 4)
        return g, ((at_y * 4 + at_x) * 2 + lax.rem(zlo + dz, 2)) * 2 + lax.rem(core + dc, 2)

    def along_z(step):
        z = lax.rem(g * 2 + zlo + step, 8)
        return z // 2, w + 2 * (lax.rem(z, 2) - zlo)

    barrier = pltpu.get_barrier_semaphore()

    def greet(to):
        pl.semaphore_signal(barrier, inc=1, device_id=to, device_id_type=MESH)

    def greet_group(o, carry):
        greet((g, w ^ o))
        return carry

    def greet_ring(step, carry):
        to = along_z(step)

        @pl.when(to[0] != g)
        def _():
            greet(to)

        return carry

    lax.fori_loop(1, 8, greet_ring, 0)
    lax.fori_loop(1, writers, greet_group, 0)
    pl.semaphore_wait(barrier, writers - 1 + 6)
    for copy in loads:
        copy.wait()

    mine = pl.ds(pl.multiple_of(w * rows, rows), rows)
    for c, (first, width) in enumerate(chunks):
        at = pl.ds(first, width)

        def source(p):
            return staged.at[:, pl.ds(pl.multiple_of(p * own + first, 128), width)]

        for o in ORDER:
            to = peer(o)
            to_peer(source(to[1]), cells_ref.at[mine, at], send.at[0], recv.at[c], to).start()
        pltpu.make_async_copy(source(w), cells_ref.at[mine, at], recv.at[c]).start()

    dot = lambda p, q: lax.dot_general(p, q, (((1,), (1,)), ((), ())), preferred_element_type=F32)
    for c, (first, width) in enumerate(chunks):
        part = cells_ref.at[:, pl.ds(first, width)]
        wait_bytes(part, recv.at[c])
        hi, mid, lo = split3(part[...])
        at = pl.ds(first, width)
        high_ref[:, at], mid_ref[:, at], low_ref[:, at] = hi, mid, lo
        small_terms = (dot(hi, lo) + dot(lo, hi) + dot(mid, mid)) + (dot(hi, mid) + dot(mid, hi))
        term = small_terms + dot(hi, hi)
        local[...] = term if c == 0 else local[...] + term

    deep = snaps // 2
    strip = deep // 16

    def rows_of(p, c):
        return pl.ds(pl.multiple_of(c * deep + p * strip, strip), strip)

    for o in FAR_FIRST:
        p, c = place ^ (o // 2), core ^ (o % 2)
        to_peer(local.at[rows_of(p, c), :], pieces.at[place * 2 + core], send.at[2], small.at[1], (g, w ^ (4 * (o // 2) + o % 2))).start()
    pieces[place * 2 + core] = local[rows_of(place, core), :]
    wait_bytes(pieces.at[pl.ds(0, 31)], small.at[1])
    layer = g * 2 + zlo
    layers[layer] = jnp.sum(pieces[...], axis=0)
    for step in RING:
        to_peer(layers.at[layer], layers.at[layer], send.at[3], small.at[2], along_z(step)).start()
    wait_bytes(layers.at[pl.ds(0, 7)], small.at[2])
    total[...] = jnp.sum(layers[...], axis=0)
    rows_out = rows_of(place, core)
    for o in FAR_FIRST:
        to_peer(total, gram_ref.at[rows_out, :], send.at[4], small.at[3], (g, w ^ (4 * (o // 2) + o % 2))).start()
    gram_ref[rows_out, :] = total[...]
    wait_bytes(gram_ref.at[pl.ds(0, 31 * strip), :], small.at[3])
    wait_bytes(staged.at[:, pl.ds(0, (writers - 1) * own)], send.at[0])
    wait_bytes(pieces.at[pl.ds(0, 31)], send.at[2])
    wait_bytes(layers.at[pl.ds(0, 7)], send.at[3])
    wait_bytes(gram_ref.at[pl.ds(0, 31 * strip), :], send.at[4])


def regroup(x):
    rows, cells = x.shape
    writers = lax.axis_size("wr")
    snaps, own = rows * writers, cells // writers
    chunks = CHUNKS
    return pl.pallas_call(
        functools.partial(regroup_kernel, chunks),
        out_shape=(*[jax.ShapeDtypeStruct((snaps, own), BF)] * 3, jax.ShapeDtypeStruct((snaps, snaps), F32)),
        in_specs=[pl.BlockSpec(memory_space=pltpu.HBM)],
        out_specs=(pl.BlockSpec(memory_space=pltpu.VMEM),) * 4,
        scratch_shapes=[
            pltpu.VMEM((snaps, own), F32),
            pltpu.VMEM((rows, cells), F32),
            pltpu.VMEM((snaps, snaps), F32),
            pltpu.VMEM((32, snaps // 32, snaps), F32),
            pltpu.VMEM((8, snaps // 32, snaps), F32),
            pltpu.VMEM((snaps // 32, snaps), F32),
            pltpu.SemaphoreType.DMA((5,)),
            pltpu.SemaphoreType.DMA((len(chunks),)),
            pltpu.SemaphoreType.DMA((4,)),
            pltpu.SemaphoreType.DMA((4,)),
        ],
        compiler_params=pltpu.CompilerParams(
            collective_id=0, has_side_effects=True, vmem_limit_bytes=46 << 20
        ),
    )(x)


def body(snapshots):
    *cells, gram = regroup(snapshots)
    basis, columns = finish(gram, cells)
    return basis, columns.T


def solution(mesh):
    return jax.shard_map(
        body,
        mesh=mesh,
        in_specs=(P("wr", "grp"),),
        out_specs=(P(None, ("grp", "wr")), P(None, "wr")),
        check_vma=False,
    )
```

```python
import functools

import jax
import jax.numpy as jnp
from jax import lax
from jax.experimental import pallas as pl
from jax.experimental.pallas import tpu as pltpu
from jax.sharding import PartitionSpec as P

F32 = jnp.float32
BF = jnp.bfloat16
MESH = pl.DeviceIdType.MESH

CHUNKS = ((0, 1920), (1920, 1152), (3072, 640), (3712, 384))

def split3(v):
    hi=v.astype(BF); r=v-hi.astype(F32); mid=r.astype(BF); lo=(r-mid.astype(F32)).astype(BF)
    return hi,mid,lo

def rsqrt_exact(d):
    y=lax.rsqrt(d)
    return y*(1.5-0.5*d*y*y)

def pick(rows, l):
    where = jnp.full(rows.shape, l, jnp.int32)
    return jnp.take_along_axis(rows, where, axis=1, mode="promise_in_bounds")


def factor(a_ref, v_ref, u_ref, b, product, rows_out):
    n=a_ref.shape[0]; halves=n//128; groups=b//8
    lane=lax.broadcasted_iota(jnp.int32,(8,128),1); row=lax.broadcasted_iota(jnp.int32,(8,128),0)
    lane_all=lax.broadcasted_iota(jnp.int32,(n,n),1)
    lane_b=lax.broadcasted_iota(jnp.int32,(b,n),1); row_b=lax.broadcasted_iota(jnp.int32,(b,n),0)
    def panel(p,carry):
        k=pl.multiple_of(p*b,b)
        product(jnp.maximum(p-1,0))
        P=pltpu.roll(a_ref[pl.ds(k,b),:],lax.rem(n-k,n),1)
        G=[[P[8*g:8*g+8,128*h:128*h+128] for h in range(halves)] for g in range(groups)]
        UD=[None]*groups
        for q in range(groups):
            W=[{g:pick(G[g][0],8*q+j) for g in range(q+(q>0),groups)} for j in range(8)]
            if q>0:
                for j in range(8): W[j][q]=ahead[j]
            if q+1<groups: ahead=[pick(G[q+1][0],8*q+8+j) for j in range(8)]
            own=(lane>=8*q)&(lane<8*q+8)
            for g in range(q,groups):
                G[g][0]=jnp.where(own,(jnp.where(lane==row+8*q,1.0,0.0) if g==q else 0.0),G[g][0])
            dv=jnp.ones((8,128),F32)
            for j in range(8):
                d=W[j][q][j:j+1,:]
                r=1.0/d
                dv=jnp.where(row==j,d,dv)
                m={g:W[j][g]*r for g in range(q,groups)}
                m[q]=jnp.where(row>j,m[q],0.0)
                for jj in range(j+1,8):
                    pv=W[jj][q][j:j+1,:]
                    for g in range(q,groups): W[jj][g]=W[jj][g]-m[g]*pv
                if q+1<groups:
                    for jj in range(8): ahead[jj]=ahead[jj]-m[q+1]*W[j][q+1][jj:jj+1,:]
                pr=[G[q][h][j:j+1,:] for h in range(halves)]
                for g in range(q,groups):
                    for h in range(halves): G[g][h]=G[g][h]-m[g]*pr[h]
            s=rsqrt_exact(dv)
            ud=jnp.zeros((8,128),F32)
            for j in range(8): ud=jnp.where((lane==8*q+j)&(row<=j),W[j][q],ud)
            UD[q]=ud*s
            for h in range(halves): G[q][h]=G[q][h]*s
        Pf=jnp.concatenate([jnp.concatenate(g,axis=1) for g in G],axis=0)
        Pn=pltpu.roll(Pf,k,1)
        h3,m3,l3=split3(jnp.where((lane_b>row_b+k)&(lane_b<k+b),0.0,Pn))
        A=jnp.concatenate([h3,h3,m3,h3,l3,m3],axis=0)
        B=jnp.concatenate([h3,m3,h3,l3,h3,m3],axis=0)
        upd=lax.dot_general(A,B,(((0,),(0,)),((),())),preferred_element_type=F32)
        inpan=(lane_all>=k)&(lane_all<k+b)
        a_ref[...]=jnp.where(inpan,0.0,a_ref[...])-upd
        blk=(row_b//8)*8
        v_ref[pl.ds(k,b),:]=jnp.where(lane_b<=row_b+k,Pn,0.0)
        UDp=jnp.concatenate([jnp.concatenate([UD[g]]+[jnp.zeros((8,128),F32)]*(halves-1),axis=1) for g in range(groups)],axis=0)
        UDn=pltpu.roll(UDp,k,1)
        u_ref[pl.ds(k,b),:]=jnp.where(lane_b>=blk+k+8,Pn,UDn)
        @pl.when(p>0)
        def _(): rows_out(p-1).start()
        return carry
    lax.fori_loop(0,n//b,panel,0)
    product(n//b-1)
    rows_out(n//b-1).start()

def finish_kernel(b, cw, g_ref, xh_ref, xm_ref, xl_ref, o_hbm, r_ref, a, v, u, ob, out_sem):
    n, cells = xh_ref.shape
    w = lax.axis_index("wr")
    a[...] = g_ref[...]
    v[0:b, :] = jnp.zeros((b, n), F32)

    def product(p):
        at = pl.ds(pl.multiple_of(p * b, b), b)
        vh, vm, vl = split3(v[at, :] * 1024.0)
        three, two = jnp.concatenate([vh, vm, vl], axis=0), jnp.concatenate([vh, vm], axis=0)
        f = lambda l, r: jnp.dot(l, r, preferred_element_type=F32)
        for i in range(cells // cw):
            part = slice(i * cw, (i + 1) * cw)
            th, tm, tl = f(three, xh_ref[:, part]), f(two, xm_ref[:, part]), f(vh, xl_ref[:, part])
            ob[at, part] = (th[2 * b :] + tm[b:] + tl) + (th[b : 2 * b] + tm[:b]) + th[:b]

    def rows_out(p):
        at = pl.ds(pl.multiple_of(p * b, b), b)
        return pltpu.make_async_copy(ob.at[at, :], o_hbm.at[at, :], out_sem.at[p])

    factor(a, v, u, b, product, rows_out)
    turned = pltpu.roll(u[...], lax.rem(n - 4 * w, n), 1)
    r_ref[...] = turned[:, 0:128].T[0:4, :] * (1.0 / 1024.0)
    for p in range(n // b):
        rows_out(p).wait()


def finish(gram, x, b=64, cw=256):
    n, cells = x[0].shape
    return pl.pallas_call(
        functools.partial(finish_kernel, b, cw),
        out_shape=(jax.ShapeDtypeStruct((n, cells), F32), jax.ShapeDtypeStruct((4, n), F32)),
        in_specs=[pl.BlockSpec(memory_space=pltpu.VMEM)] * 4,
        out_specs=(pl.BlockSpec(memory_space=pltpu.HBM), pl.BlockSpec(memory_space=pltpu.VMEM)),
        scratch_shapes=[pltpu.VMEM((n, n), F32)] * 3 + [pltpu.VMEM((n, cells), F32), pltpu.SemaphoreType.DMA((n // b,))],
        compiler_params=pltpu.CompilerParams(vmem_limit_bytes=40 << 20),
    )(gram, *x)


def to_peer(src, dst, send_sem, recv_sem, peer):
    return pltpu.make_async_remote_copy(
        src_ref=src, dst_ref=dst, send_sem=send_sem, recv_sem=recv_sem, device_id=peer, device_id_type=MESH
    )


def wait_bytes(ref, sem):
    pltpu.make_async_copy(ref, ref, sem).wait()


ORDER = (
    (0, 3, 1, 1),
    (2, 1, 1, 0),
    (3, 3, 0, 0),
    (0, 1, 1, 0),
    (2, 3, 0, 0),
    (0, 2, 0, 0),
    (1, 0, 1, 1),
    (3, 1, 0, 0),
    (2, 2, 1, 0),
    (1, 0, 1, 0),
    (3, 2, 0, 0),
    (2, 2, 1, 1),
    (2, 3, 1, 0),
    (0, 1, 0, 0),
    (0, 0, 0, 1),
    (2, 3, 0, 1),
    (3, 3, 1, 0),
    (1, 1, 1, 1),
    (1, 2, 0, 0),
    (3, 0, 1, 1),
    (2, 2, 0, 0),
    (0, 1, 0, 1),
    (0, 3, 1, 0),
    (2, 0, 0, 0),
    (0, 0, 1, 0),
    (2, 1, 0, 1),
    (0, 3, 0, 0),
    (0, 1, 1, 1),
    (3, 3, 0, 1),
    (2, 0, 1, 1),
    (1, 2, 0, 1),
    (3, 2, 1, 0),
    (1, 1, 1, 0),
    (2, 3, 1, 1),
    (0, 2, 0, 1),
    (3, 0, 0, 1),
    (1, 3, 0, 0),
    (3, 1, 1, 0),
    (1, 0, 0, 0),
    (3, 1, 0, 1),
    (1, 3, 1, 0),
    (3, 2, 0, 1),
    (1, 2, 1, 1),
    (0, 0, 1, 1),
    (3, 0, 0, 0),
    (1, 3, 0, 1),
    (2, 1, 1, 1),
    (0, 2, 1, 1),
    (2, 1, 0, 0),
    (0, 3, 0, 1),
    (3, 0, 1, 0),
    (1, 3, 1, 1),
    (1, 1, 0, 0),
    (1, 2, 1, 0),
    (2, 2, 0, 1),
    (3, 3, 1, 1),
    (3, 1, 1, 1),
    (2, 0, 0, 1),
    (0, 2, 1, 0),
    (1, 0, 0, 1),
    (3, 2, 1, 1),
    (1, 1, 0, 1),
    (2, 0, 1, 0),
)
RING = (4, 3, 5, 2, 6, 1, 7)
HOPS = (0, 1, 2, 1)
FAR_FIRST = sorted(range(1, 32), key=lambda o: -HOPS[o // 8] - HOPS[o // 2 % 4])


def regroup_kernel(chunks, x_hbm, high_ref, mid_ref, low_ref, gram_ref, cells_ref, staged, local, pieces, layers, total, send, recv, small, load):
    g, w = lax.axis_index("grp"), lax.axis_index("wr")
    snaps, own = cells_ref.shape
    rows = x_hbm.shape[0]
    writers = snaps // rows
    core, zlo, place = lax.rem(w, 2), lax.rem(w // 2, 2), w // 4
    x, y = lax.rem(place, 4), place // 4

    pieces_in = 4
    span = x_hbm.shape[1] // pieces_in
    loads = [
        pltpu.make_async_copy(x_hbm.at[:, pl.ds(i * span, span)], staged.at[:, pl.ds(i * span, span)], load.at[i])
        for i in range(pieces_in)
    ]
    for copy in loads:
        copy.start()

    def peer(offset):
        dy, dx, dz, dc = offset
        at_y, at_x = lax.rem(y + dy, 4), lax.rem(x + dx, 4)
        return g, ((at_y * 4 + at_x) * 2 + lax.rem(zlo + dz, 2)) * 2 + lax.rem(core + dc, 2)

    def along_z(step):
        z = lax.rem(g * 2 + zlo + step, 8)
        return z // 2, w + 2 * (lax.rem(z, 2) - zlo)

    barrier = pltpu.get_barrier_semaphore()

    def greet(to):
        pl.semaphore_signal(barrier, inc=1, device_id=to, device_id_type=MESH)

    def greet_group(o, carry):
        greet((g, w ^ o))
        return carry

    def greet_ring(step, carry):
        to = along_z(step)

        @pl.when(to[0] != g)
        def _():
            greet(to)

        return carry

    lax.fori_loop(1, 8, greet_ring, 0)
    lax.fori_loop(1, writers, greet_group, 0)
    pl.semaphore_wait(barrier, writers - 1 + 6)
    for copy in loads:
        copy.wait()

    mine = pl.ds(pl.multiple_of(w * rows, rows), rows)
    for c, (first, width) in enumerate(chunks):
        at = pl.ds(first, width)

        def source(p):
            return staged.at[:, pl.ds(pl.multiple_of(p * own + first, 128), width)]

        for o in ORDER:
            to = peer(o)
            to_peer(source(to[1]), cells_ref.at[mine, at], send.at[0], recv.at[c], to).start()
        pltpu.make_async_copy(source(w), cells_ref.at[mine, at], recv.at[c]).start()

    dot = lambda p, q: lax.dot_general(p, q, (((1,), (1,)), ((), ())), preferred_element_type=F32)
    for c, (first, width) in enumerate(chunks):
        part = cells_ref.at[:, pl.ds(first, width)]
        wait_bytes(part, recv.at[c])
        hi, mid, lo = split3(part[...])
        at = pl.ds(first, width)
        high_ref[:, at], mid_ref[:, at], low_ref[:, at] = hi, mid, lo
        small_terms = (dot(hi, lo) + dot(lo, hi) + dot(mid, mid)) + (dot(hi, mid) + dot(mid, hi))
        term = small_terms + dot(hi, hi)
        local[...] = term if c == 0 else local[...] + term

    deep = snaps // 2
    strip = deep // 16

    def rows_of(p, c):
        return pl.ds(pl.multiple_of(c * deep + p * strip, strip), strip)

    for o in FAR_FIRST:
        p, c = place ^ (o // 2), core ^ (o % 2)
        to_peer(local.at[rows_of(p, c), :], pieces.at[place * 2 + core], send.at[2], small.at[1], (g, w ^ (4 * (o // 2) + o % 2))).start()
    pieces[place * 2 + core] = local[rows_of(place, core), :]
    wait_bytes(pieces.at[pl.ds(0, 31)], small.at[1])
    layer = g * 2 + zlo
    layers[layer] = jnp.sum(pieces[...], axis=0)
    for step in RING:
        to_peer(layers.at[layer], layers.at[layer], send.at[3], small.at[2], along_z(step)).start()
    wait_bytes(layers.at[pl.ds(0, 7)], small.at[2])
    total[...] = jnp.sum(layers[...], axis=0)
    rows_out = rows_of(place, core)
    for o in FAR_FIRST:
        to_peer(total, gram_ref.at[rows_out, :], send.at[4], small.at[3], (g, w ^ (4 * (o // 2) + o % 2))).start()
    gram_ref[rows_out, :] = total[...]
    wait_bytes(gram_ref.at[pl.ds(0, 31 * strip), :], small.at[3])
    wait_bytes(staged.at[:, pl.ds(0, (writers - 1) * own)], send.at[0])
    wait_bytes(pieces.at[pl.ds(0, 31)], send.at[2])
    wait_bytes(layers.at[pl.ds(0, 7)], send.at[3])
    wait_bytes(gram_ref.at[pl.ds(0, 31 * strip), :], send.at[4])


def regroup(x):
    rows, cells = x.shape
    writers = lax.axis_size("wr")
    snaps, own = rows * writers, cells // writers
    chunks = CHUNKS
    return pl.pallas_call(
        functools.partial(regroup_kernel, chunks),
        out_shape=(*[jax.ShapeDtypeStruct((snaps, own), BF)] * 3, jax.ShapeDtypeStruct((snaps, snaps), F32)),
        in_specs=[pl.BlockSpec(memory_space=pltpu.HBM)],
        out_specs=(pl.BlockSpec(memory_space=pltpu.VMEM),) * 4,
        scratch_shapes=[
            pltpu.VMEM((snaps, own), F32),
            pltpu.VMEM((rows, cells), F32),
            pltpu.VMEM((snaps, snaps), F32),
            pltpu.VMEM((32, snaps // 32, snaps), F32),
            pltpu.VMEM((8, snaps // 32, snaps), F32),
            pltpu.VMEM((snaps // 32, snaps), F32),
            pltpu.SemaphoreType.DMA((5,)),
            pltpu.SemaphoreType.DMA((len(chunks),)),
            pltpu.SemaphoreType.DMA((4,)),
            pltpu.SemaphoreType.DMA((4,)),
        ],
        compiler_params=pltpu.CompilerParams(
            collective_id=0, has_side_effects=True, vmem_limit_bytes=46 << 20
        ),
    )(x)


def body(snapshots):
    *cells, gram = regroup(snapshots)
    basis, columns = finish(gram, cells)
    return basis, columns.T


def solution(mesh):
    return jax.shard_map(
        body,
        mesh=mesh,
        in_specs=(P("wr", "grp"),),
        out_specs=(P(None, ("grp", "wr")), P(None, "wr")),
        check_vma=False,
    )
```
